128 devices in a mesh: dp: 8 (over z, core), tensor: 16 (over y, x).
Axes of the slice: x: 4, y: 4, z: 4, core: 2. Of those that a mesh axis runs over, the one named last changes fastest.
Arguments:
- tokens: bfloat16 [2048, 4096], P('dp', 'tensor'), may hold values from -6 to 6
- gate_pre: bfloat16 [2048, 14336], P('dp', 'tensor'), may hold values from -8 to 8
- up_act: bfloat16 [2048, 14336], P('dp', 'tensor'), may hold values from -6 to 6
- grad_hidden: bfloat16 [2048, 14336], P('dp', 'tensor'), may hold values from -1 to 1
- gate_weight: bfloat16 [4096, 14336], P(None, 'tensor'), may hold values from -0.09375 to 0.09375
- up_weight: bfloat16 [4096, 14336], P(None, 'tensor'), may hold values from -0.09375 to 0.09375
- q_init: float32 [14336, 64], P('tensor'), may hold values from -6 to 6
Outputs:
- grad_input: bfloat16 [2048, 4096], P('dp')
- gate_q: float32 [14336, 64], P('tensor')
- gate_error: bfloat16 [32768, 14336], P('dp', 'tensor')
The draws below stay inside these ranges and needn't reach their ends.
All inputs are finite; a program needn't handle non-finite values.
Results may differ from the reference program's by a relative error of at most 0.0075.
Values may be sent and summed in bfloat16 or wider, within the bound.
No kernel may reach another device: no remote copies, remote signals or barrier semaphores. Data moves between devices by JAX's collectives and lax.ppermute only.
A program may use at most 128 MiB of HBM per device.

```python
import jax
import jax.numpy as jnp
from jax import lax

D = 4096
FF = 14336
R = 64
TOK_DEV = 256
TOKENS = 2048
N_DP = 8
N_TENSOR = 16


def steps_of(key, dims, pieces, least, high):
    def one(position, shards_of):
        steps = jax.random.uniform(jax.random.fold_in(jax.random.fold_in(key, 6), position), (shards_of,), jnp.float32, least / len(pieces), high / len(pieces))
        return jnp.repeat(jnp.exp(steps), dims[position] // shards_of).reshape((-1,) + (1,) * (len(dims) - position - 1))

    loudness = one(*pieces[0])
    for cut in pieces[1:]:
        loudness = loudness * one(*cut)
    return loudness


def scatter_about(stream_key, extent, spread, bound, cuts=(), kind=jnp.bfloat16):
    entries = spread * jax.random.normal(stream_key, extent, jnp.float32)
    if cuts:
        entries = entries * steps_of(stream_key, extent, cuts, -0.22, 0.18)
    return jnp.clip(entries, -bound, bound).astype(kind)


def setup_inputs(seed: int = 0) -> dict:
    seeds = jax.random.split(jax.random.key(seed), 8)
    return {
        "tokens": scatter_about(seeds[0], (TOKENS, D), 1.0, 6.0, ((0, 8), (1, 16))),
        "gate_pre": scatter_about(seeds[1], (TOKENS, FF), 1.5, 8.0, ((0, 8), (1, 16))),
        "up_act": scatter_about(seeds[2], (TOKENS, FF), 1.0, 6.0, ((0, 8), (1, 16))),
        "grad_hidden": scatter_about(seeds[3], (TOKENS, FF), 0.125, 1.0, ((0, 8), (1, 16))),
        "gate_weight": scatter_about(seeds[4], (D, FF), D ** -0.5, 0.09375, ((1, 16),)),
        "up_weight": scatter_about(seeds[5], (D, FF), D ** -0.5, 0.09375, ((1, 16),)),
        "q_init": scatter_about(seeds[6], (FF, R), 1.0, 6.0, ((0, 16),), jnp.float32),
    }


def gram_schmidt(factor):
    highest = lax.Precision.HIGHEST

    def column_step(column_id, orthonormal):
        column = lax.dynamic_slice_in_dim(factor, column_id, 1, 1)
        weights_col = jnp.dot(orthonormal.T, column, precision=highest)
        vector = column - jnp.dot(orthonormal, weights_col, precision=highest)
        vector = vector / jnp.sqrt(jnp.sum(vector * vector))
        return lax.dynamic_update_slice_in_dim(orthonormal, vector, column_id, 1)
    return lax.fori_loop(0, factor.shape[1], column_step, jnp.zeros_like(factor))

def reference(tokens, gate_pre, up_act, grad_hidden, gate_weight, up_weight, q_init):
    highest = lax.Precision.HIGHEST
    preact = gate_pre.astype(jnp.float32)
    sigmoid_gate = jax.nn.sigmoid(preact)
    cotangent = grad_hidden.astype(jnp.float32)
    grad_up = (cotangent * preact * sigmoid_gate).astype(jnp.bfloat16)
    grad_gate = (cotangent * up_act.astype(jnp.float32) * sigmoid_gate * (1.0 + preact * (1.0 - sigmoid_gate))).astype(jnp.bfloat16)
    contract_last = (((1,), (1,)), ((), ()))
    summed = lax.dot_general(grad_gate, gate_weight, contract_last, preferred_element_type=jnp.float32)
    summed = summed + lax.dot_general(grad_up, up_weight, contract_last, preferred_element_type=jnp.float32)
    grad_input = summed.astype(jnp.bfloat16)
    shard_width = FF // N_TENSOR
    features = tokens.astype(jnp.float32).reshape(N_DP, TOK_DEV, D)
    gate_shards = grad_gate.reshape(N_DP, TOK_DEV, N_TENSOR, shard_width).transpose(2, 0, 1, 3)
    q_shards = q_init.reshape(N_TENSOR, shard_width, R)

    def shard_work(inputs):
        shard_gate, shard_q = inputs
        gradient = jnp.einsum('ntd,ntf->ndf', features, shard_gate.astype(jnp.float32), precision=highest)
        left_sum = lax.optimization_barrier(jnp.sum(jnp.einsum('ndf,fr->ndr', gradient, shard_q, precision=highest), axis=0))
        orthonormal = gram_schmidt(left_sum)
        right_mean = lax.optimization_barrier(jnp.sum(jnp.einsum('ndf,dr->nfr', gradient, orthonormal, precision=highest), axis=0)) / N_DP
        rebuilt = jnp.dot(orthonormal, right_mean.T, precision=highest)
        residual = (gradient - rebuilt[None]).astype(jnp.bfloat16)
        return (residual, right_mean)
    residuals, right_means = lax.map(shard_work, (gate_shards, q_shards))
    gate_error = residuals.transpose(1, 2, 0, 3).reshape(N_DP * D, FF)
    gate_q = right_means.reshape(FF, R)
    return (grad_input, gate_q, gate_error)
```

```python
import jax
import jax.numpy as jnp
from jax import lax
from jax.experimental import pallas as pl
from jax.experimental.pallas import tpu as pltpu
from jax.sharding import PartitionSpec as P

F32 = jnp.float32
BF16 = jnp.bfloat16
SIDE = 4
MIB = 1024 * 1024


def mm(a, b, ca, cb):
    return lax.dot_general(a, b, (((ca,), (cb,)), ((), ())), preferred_element_type=F32)


def mm_exact(a, b, ca, cb):
    return lax.dot_general(
        a, b, (((ca,), (cb,)), ((), ())),
        precision=lax.Precision.HIGHEST, preferred_element_type=F32,
    )


def split_hi_lo(a):
    hi = a.astype(BF16)
    return hi, (a - hi.astype(F32)).astype(BF16)


def vmem():
    return pl.BlockSpec(memory_space=pltpu.VMEM)


def smem():
    return pl.BlockSpec(memory_space=pltpu.SMEM)


def call(kernel, outs, n_in, flops, nbytes, scratch=(), mib=32, scalars=1):
    return pl.pallas_call(
        kernel,
        out_shape=outs,
        in_specs=[smem()] * scalars + [vmem()] * n_in,
        out_specs=jax.tree.map(lambda _: vmem(), outs),
        scratch_shapes=list(scratch),
        compiler_params=pltpu.CompilerParams(vmem_limit_bytes=mib * MIB),
        cost_estimate=pl.CostEstimate(flops=flops, bytes_accessed=nbytes, transcendentals=0),
    )


def shape(*dims, dtype=BF16):
    return jax.ShapeDtypeStruct(dims, dtype)


def gates_kernel(pos, gate_pre, up_act, grad_hidden, q_t, gate, rel, z_t):
    x, y = pos[0], pos[1]
    width = gate_pre.shape[1]
    rows = gate_pre.shape[0] // (SIDE * SIDE)
    for k in range(SIDE):
        for j in range(SIDE):
            src = ((x + k) % SIDE) * SIDE + (y + j) % SIDE
            src = pl.ds(pl.multiple_of(src * rows, rows), rows)
            dst = pl.ds((k * SIDE + j) * rows, rows)
            pre = gate_pre[src, :].astype(F32)
            cot = grad_hidden[src, :].astype(F32)
            sig = 1.0 / (1.0 + jnp.exp(-pre))
            rel[dst, width:] = (cot * pre * sig).astype(BF16)
            grad_gate = (
                cot * up_act[src, :].astype(F32) * sig * (1.0 + pre * (1.0 - sig))
            ).astype(BF16)
            rel[dst, :width] = grad_gate
            gate[src, :] = grad_gate
    q_hi, q_lo = split_hi_lo(q_t[...])
    z = mm(jnp.concatenate([q_hi, q_lo], 0), gate[...], 1, 1)
    r = q_t.shape[0]
    z_hi, z_lo = split_hi_lo(z[:r] + z[r:])
    z_t[:r] = z_hi
    z_t[r:] = z_lo


def partial_kernel(rel, gate_weight, up_weight, *outs):
    width = gate_weight.shape[1]
    acc = mm(rel[:, :width], gate_weight[...], 1, 1)
    acc = acc + mm(rel[:, width:], up_weight[...], 1, 1)
    rows = acc.shape[0] // SIDE
    for k in range(SIDE):
        outs[k][...] = acc[k * rows:(k + 1) * rows].astype(outs[k].dtype)


def partial_input(rel, gate_weight, up_weight):
    tokens, both = rel.shape
    d, width = gate_weight.shape
    block = 512
    rows = tokens // SIDE
    return pl.pallas_call(
        partial_kernel,
        grid=(d // block,),
        in_specs=[
            pl.BlockSpec((tokens, both), lambda i: (0, 0)),
            pl.BlockSpec((block, width), lambda i: (i, 0)),
            pl.BlockSpec((block, width), lambda i: (i, 0)),
        ],
        out_specs=[pl.BlockSpec((rows, block), lambda i: (0, i))] * SIDE,
        out_shape=[shape(rows, d, dtype=F32)] + [shape(rows, d)] * (SIDE - 1),
        compiler_params=pltpu.CompilerParams(vmem_limit_bytes=24 * MIB),
        cost_estimate=pl.CostEstimate(
            flops=2 * tokens * both * d, bytes_accessed=4 * d * width, transcendentals=0
        ),
    )(rel, gate_weight, up_weight)


def sum_split_kernel(own, a, b, c, *outs):
    rows = own.shape[0] // SIDE
    for j in range(SIDE):
        cut = pl.ds(j * rows, rows)
        total = (own[cut, :] + a[cut, :].astype(F32)) + (b[cut, :].astype(F32) + c[cut, :].astype(F32))
        outs[j][...] = total.astype(outs[j].dtype)


def sum_kernel(own, a, b, c, out):
    total = (own[...].astype(F32) + b[...].astype(F32)) + (a[...].astype(F32) + c[...].astype(F32))
    out[...] = total.astype(out.dtype)


def place_kernel(which, pos, own, a, b, c, out):
    rows = own.shape[0]
    for k, block in enumerate((own, a, b, c)):
        at = (pos[which] + SIDE - k) % SIDE
        out[pl.ds(pl.multiple_of(at * rows, rows), rows), :] = block[...]


def left_kernel(pos, z_t, t0, t1, t2, t3, keep, send):
    core = pos[2]
    r = keep.shape[0]
    cols = t0.shape[2]
    for j, stack in enumerate((t0, t1, t2, t3)):
        half, base = j // 2, (j % 2) * SIDE * cols

        def emit(target):
            for k in range(SIDE):
                part = mm(z_t[...], stack[k], 1, 0)
                target[:, base + k * cols:base + (k + 1) * cols] = (
                    part[:r] + part[r:]
                ).astype(target.dtype)

        pl.when(core == half)(lambda: emit(keep))
        pl.when(core != half)(lambda: emit(send))


def right_kernel(pos, mine, other, gate, t0, t1, t2, t3, left, v_t, gram):
    core = pos[2]
    left[core] = mine[...]
    left[1 - core] = other[...]
    r = mine.shape[0]
    cols = t0.shape[2]
    w = jnp.zeros((gate.shape[0], r), F32)
    c = jnp.zeros((r, r), F32)
    for j, stack in enumerate((t0, t1, t2, t3)):
        for k in range(SIDE):
            at = (j % 2) * SIDE * cols + k * cols
            piece = left[j // 2, :, at:at + cols]
            w = w + mm(stack[k], piece, 1, 1)
            c = c + mm(piece, piece, 1, 1)
    gram[...] = c
    w_hi, w_lo = split_hi_lo(w)
    v = mm(jnp.concatenate([w_hi, w_lo], 1), gate[...], 0, 0)
    v_t[...] = v[:r] + v[r:]


def cholesky_kernel(gram, out):
    r = gram.shape[0]
    row_id = lax.broadcasted_iota(jnp.int32, (r, 2 * r), 0)
    lane_id = lax.broadcasted_iota(jnp.int32, (r, 2 * r), 1)
    eye = jnp.where(row_id + r == lane_id, 1.0, 0.0).astype(F32)
    a = jnp.concatenate([gram[...], jnp.zeros((r, r), F32)], 1) + eye
    for k in range(r):
        row = a[k:k + 1, :]
        col = a[:, k:k + 1]
        pivot = a[k:k + 1, k:k + 1]
        scale = jnp.where(row_id[:, :1] > k, col / pivot, 0.0)
        a = a - scale * row
    diag = jnp.sum(jnp.where(row_id == lane_id, a, 0.0), axis=1, keepdims=True)
    out[...] = a[:, r:] / jnp.sqrt(diag)


def residual_kernel(n_dp, slots, pos, v_t, inv, gate, left, t0, t1, t2, t3, gate_q_t, out, right):
    step = pl.program_id(0)
    r = v_t.shape[0]

    @pl.when(step == 0)
    def _():
        q = mm_exact(inv[...], v_t[...], 1, 0) * (1.0 / n_dp)
        gate_q_t[...] = q
        hi, lo = split_hi_lo(-mm_exact(inv[...], q, 0, 0))
        right[:r] = hi
        right[r:] = lo

    j, k = step // SIDE, step % SIDE
    cols = t0.shape[2]
    at = pl.multiple_of((j % 2) * SIDE * cols + k * cols, cols)
    piece = left[j // 2, :, pl.ds(at, cols)]
    low = mm(jnp.concatenate([piece, piece], 0), right[...], 0, 0)
    for n, stack in enumerate((t0, t1, t2, t3)):
        @pl.when(j == n)
        def _():
            out[...] = (mm(stack[k], gate[...], 0, 0) + low).astype(out.dtype)


def residual(slots, v_t, inv, gate, left, stacks, n_dp):
    r, width = v_t.shape
    tokens = gate.shape[0]
    cols = stacks[0].shape[2]
    n = SIDE * SIDE
    whole = lambda a: pl.BlockSpec(a.shape, lambda i, s, nd=a.ndim: (0,) * nd)
    ins = (v_t, inv, gate, left, *stacks)

    def kernel(slots_ref, *refs):
        residual_kernel(n_dp, slots_ref, None, *refs)

    return pl.pallas_call(
        kernel,
        grid_spec=pltpu.PrefetchScalarGridSpec(
            num_scalar_prefetch=1,
            grid=(n,),
            in_specs=[whole(a) for a in ins],
            out_specs=[
                pl.BlockSpec((r, width), lambda i, s: (0, 0)),
                pl.BlockSpec((cols, width), lambda i, s: (s[i], 0)),
            ],
            scratch_shapes=[pltpu.VMEM((2 * r, width), BF16)],
        ),
        out_shape=[shape(r, width, dtype=F32), shape(n * cols, width)],
        compiler_params=pltpu.CompilerParams(vmem_limit_bytes=32 * MIB),
        cost_estimate=pl.CostEstimate(
            flops=2 * n * cols * width * (tokens + 2 * r),
            bytes_accessed=2 * n * cols * width,
            transcendentals=0,
        ),
    )(slots, *ins)


def plane(dx, dy):
    return [
        (y * SIDE + x, ((y + dy) % SIDE) * SIDE + (x + dx) % SIDE)
        for y in range(SIDE)
        for x in range(SIDE)
    ]


def local(tokens, gate_pre, up_act, grad_hidden, gate_weight, up_weight, q_init):
    n_dp = lax.axis_size("dp")
    me = lax.axis_index("tensor")
    x, y = me % SIDE, me // SIDE
    core = lax.axis_index("dp") % 2
    pos = jnp.stack([x, y, core]).astype(jnp.int32)
    steps = jnp.arange(SIDE * SIDE, dtype=jnp.int32)
    slots = ((y - steps // SIDE) % SIDE) * SIDE + (x - steps % SIDE) % SIDE
    t_tok, width = gate_pre.shape
    r = q_init.shape[1]
    d = gate_weight.shape[0]

    def over_x(a, k):
        return lax.ppermute(a, "tensor", plane(k, 0))

    def over_y(a, j):
        return lax.ppermute(a, "tensor", plane(0, j))

    def over_z(a, k):
        return lax.ppermute(a, "dp", [(i, (i + 2 * k) % n_dp) for i in range(n_dp)])

    def over_core(a):
        return lax.ppermute(a, "dp", [(i, i ^ 1) for i in range(n_dp)])

    shifts = (1, 3, 2)

    got = {k: over_x(tokens, k) for k in shifts}
    stack0 = jnp.stack([tokens, got[1], got[2], got[3]])
    far = {j: over_y(stack0, j) for j in shifts}
    stacks = (stack0, far[1], far[2], far[3])

    gate, rel, z_t = call(
        gates_kernel,
        [shape(t_tok, width), shape(t_tok, 2 * width), shape(2 * r, t_tok)],
        4, 2 * t_tok * width * 2 * r, 8 * t_tok * width,
    )(pos, gate_pre, up_act, grad_hidden, q_init.T)

    parts = partial_input(rel, gate_weight, up_weight)
    got = {k: over_x(parts[k], k) for k in shifts}
    sums = call(
        sum_split_kernel,
        [shape(t_tok // 16, d, dtype=F32)] + [shape(t_tok // 16, d)] * 3,
        4, 4 * t_tok * d, 4 * t_tok * d, scalars=0,
    )(parts[0], got[1], got[2], got[3])
    got = {j: over_y(sums[j], j) for j in shifts}
    piece = call(
        sum_kernel, shape(t_tok // 16, d), 4, t_tok * d, t_tok * d, scalars=0
    )(sums[0], got[1], got[2], got[3])
    got = {j: over_y(piece, j) for j in shifts}
    quarter = call(
        lambda *refs: place_kernel(1, *refs), shape(t_tok // 4, d), 4, 0, t_tok * d
    )(pos, piece, got[1], got[2], got[3])
    got = {k: over_x(quarter, k) for k in shifts}
    grad_input = call(
        lambda *refs: place_kernel(0, *refs), shape(t_tok, d), 4, 0, 4 * t_tok * d
    )(pos, quarter, got[1], got[2], got[3])

    keep, send = call(
        left_kernel,
        [shape(r, d // 2, dtype=F32), shape(r, d // 2)],
        5, 2 * t_tok * d * 2 * r, 2 * t_tok * d,
    )(pos, z_t, *stacks)
    pair = (keep + over_core(send).astype(F32)).astype(BF16)
    got = {k: over_z(pair, k) for k in shifts}
    mine = call(sum_kernel, shape(r, d // 2), 4, r * d, 4 * r * d, scalars=0)(
        pair, got[1], got[2], got[3]
    )
    other = over_core(mine)

    left, v_t, gram = call(
        right_kernel,
        [shape(2, r, d // 2), shape(r, width, dtype=F32), shape(r, r, dtype=F32)],
        7, 2 * t_tok * d * r, 2 * t_tok * d,
    )(pos, mine, other, gate, *stacks)
    inv = call(
        cholesky_kernel, shape(r, r, dtype=F32), 1, 10 * MIB, r * r * 4, scalars=0
    )(gram)

    half = r // 2
    keep = lax.dynamic_slice_in_dim(v_t, core * half, half, 0)
    send = lax.dynamic_slice_in_dim(v_t, (1 - core) * half, half, 0)
    pair = keep + over_core(send)
    got = {k: over_z(pair, k) for k in shifts}
    mine = (pair + got[2]) + (got[1] + got[3])
    other = over_core(mine)
    v_sum = jnp.where(
        core == 0, jnp.concatenate([mine, other], 0), jnp.concatenate([other, mine], 0)
    )
    gate_q_t, error = residual(slots.astype(jnp.int32), v_sum, inv, gate, left, stacks, n_dp)
    return (grad_input, gate_q_t.T, error)


def solution(mesh):
    return jax.shard_map(
        local,
        mesh=mesh,
        in_specs=(
            P("dp", "tensor"),
            P("dp", "tensor"),
            P("dp", "tensor"),
            P("dp", "tensor"),
            P(None, "tensor"),
            P(None, "tensor"),
            P("tensor", None),
        ),
        out_specs=(P("dp", None), P("tensor", None), P("dp", "tensor")),
        check_vma=False,
    )
```

```python
import jax
import jax.numpy as jnp
from jax import lax
from jax.experimental import pallas as pl
from jax.experimental.pallas import tpu as pltpu
from jax.sharding import PartitionSpec as P

F32 = jnp.float32
BF16 = jnp.bfloat16
SIDE = 4
MIB = 1024 * 1024


def mm(a, b, ca, cb):
    return lax.dot_general(a, b, (((ca,), (cb,)), ((), ())), preferred_element_type=F32)


def mm_exact(a, b, ca, cb):
    return lax.dot_general(
        a, b, (((ca,), (cb,)), ((), ())),
        precision=lax.Precision.HIGHEST, preferred_element_type=F32,
    )


def split_hi_lo(a):
    hi = a.astype(BF16)
    return hi, (a - hi.astype(F32)).astype(BF16)


def vmem():
    return pl.BlockSpec(memory_space=pltpu.VMEM)


def hbm():
    return pl.BlockSpec(memory_space=pl.ANY)


def smem():
    return pl.BlockSpec(memory_space=pltpu.SMEM)


def call(kernel, outs, ins, flops, nbytes, scratch=(), mib=32, pos=None, after=()):
    lead = 0 if pos is None else 1
    several = isinstance(outs, (list, tuple))

    def body(*refs):
        kernel(*refs[:lead + len(ins)], *refs[lead + len(ins) + len(after):])

    specs = [x[0] if isinstance(x, tuple) else vmem() for x in ins]
    arrays = [x[1] if isinstance(x, tuple) else x for x in ins]
    return pl.pallas_call(
        body,
        out_shape=outs,
        in_specs=[smem()] * lead + specs + [hbm()] * len(after),
        out_specs=[vmem()] * len(outs) if several else vmem(),
        scratch_shapes=list(scratch),
        compiler_params=pltpu.CompilerParams(vmem_limit_bytes=mib * MIB),
        cost_estimate=pl.CostEstimate(flops=flops, bytes_accessed=nbytes, transcendentals=0),
    )(*([pos] if lead else []), *arrays, *after)


def shape(*dims, dtype=BF16):
    return jax.ShapeDtypeStruct(dims, dtype)


def gates_kernel(pos, pre_hbm, up_hbm, cot_hbm, q_t, gate, rel, z_t, pre_v, up_v, cot_v, sems):
    copies = [
        pltpu.make_async_copy(src, dst, sems.at[n])
        for n, (src, dst) in enumerate(((pre_hbm, pre_v), (up_hbm, up_v), (cot_hbm, cot_v)))
    ]
    for copy in copies:
        copy.start()
    for copy in copies:
        copy.wait()
    a, b = pos[0], pos[1]
    tokens, width = pre_v.shape
    rows = tokens // (SIDE * SIDE)
    for k in range(SIDE):
        for j in range(SIDE):
            src = ((a + k) % SIDE) * SIDE + (b + j) % SIDE
            src = pl.ds(pl.multiple_of(src * rows, rows), rows)
            dst = pl.ds((k * SIDE + j) * rows, rows)
            pre = pre_v[src, :].astype(F32)
            cot = cot_v[src, :].astype(F32)
            sig = 1.0 / (1.0 + jnp.exp(-pre))
            rel[dst, width:] = (cot * pre * sig).astype(BF16)
            grad_gate = (
                cot * up_v[src, :].astype(F32) * sig * (1.0 + pre * (1.0 - sig))
            ).astype(BF16)
            rel[dst, :width] = grad_gate
            gate[src, :] = grad_gate
    q_hi, q_lo = split_hi_lo(q_t[...])
    z = mm(jnp.concatenate([q_hi, q_lo], 0), gate[...], 1, 1)
    r = q_t.shape[0]
    z_hi, z_lo = split_hi_lo(z[:r] + z[r:])
    z_t[:r] = z_hi
    z_t[r:] = z_lo


def partial_kernel(rel, gate_hbm, up_hbm, o0, o1, o2, o3, gate_v, up_v, sems):
    blocks = sems.shape[0]
    d, width = gate_v.shape
    block = d // blocks

    def copies(i):
        at = pl.ds(pl.multiple_of(i * block, block), block)
        return (
            pltpu.make_async_copy(gate_hbm.at[at], gate_v.at[at], sems.at[i, 0]),
            pltpu.make_async_copy(up_hbm.at[at], up_v.at[at], sems.at[i, 1]),
        )

    for i in range(blocks):
        for copy in copies(i):
            copy.start()

    def step(i, carry):
        for copy in copies(i):
            copy.wait()
        at = pl.ds(pl.multiple_of(i * block, block), block)
        acc = mm(rel[:, :width], gate_v[at, :], 1, 1) + mm(rel[:, width:], up_v[at, :], 1, 1)
        rows = acc.shape[0] // SIDE
        for k, out in enumerate((o0, o1, o2, o3)):
            out[:, at] = acc[k * rows:(k + 1) * rows].astype(out.dtype)
        return carry

    lax.fori_loop(0, blocks, step, 0)


def stack_kernel(own, a, b, c, out):
    for k, block in enumerate((own, a, b, c)):
        out[k] = block[...]


def sum_split_kernel(own, a, b, c, *outs):
    rows = own.shape[0] // SIDE
    for j in range(SIDE):
        cut = pl.ds(j * rows, rows)
        total = (own[cut, :] + a[cut, :].astype(F32)) + (b[cut, :].astype(F32) + c[cut, :].astype(F32))
        outs[j][...] = total.astype(outs[j].dtype)


def sum_kernel(own, a, b, c, out):
    total = (own[...].astype(F32) + b[...].astype(F32)) + (a[...].astype(F32) + c[...].astype(F32))
    out[...] = total.astype(out.dtype)


def add_kernel(one, two, out):
    out[...] = (one[...].astype(F32) + two[...].astype(F32)).astype(out.dtype)


def place_kernel(which, pos, own, a, b, c, out):
    rows = own.shape[0]
    for k, block in enumerate((own, a, b, c)):
        at = (pos[which] + SIDE - k) % SIDE
        out[pl.ds(pl.multiple_of(at * rows, rows), rows), :] = block[...]


def column_block(pos, j, k):
    first, second = (pos[0] + SIDE - k) % SIDE, (pos[1] + SIDE - j) % SIDE
    return jnp.where(pos[2] == 0, second * SIDE + first, first * SIDE + second)


def left_kernel(pos, z_t, t0, t1, t2, t3, keep, send, whole):
    half, r = keep.shape[0], keep.shape[1]
    for j, stack in enumerate((t0, t1, t2, t3)):
        for k in range(SIDE):
            part = mm(z_t[...], stack[k], 1, 0)
            whole[column_block(pos, j, k)] = part[:r] + part[r:]
    keep[...] = whole[pl.ds(pos[2] * half, half)]
    send[...] = whole[pl.ds((1 - pos[2]) * half, half)].astype(send.dtype)


def turn_kernel(pos, t0, t1, t2, t3, out):
    for j, stack in enumerate((t0, t1, t2, t3)):
        for k in range(SIDE):
            out[column_block(pos, j, k)] = stack[k].T


def right_kernel(pos, mine, other, gate, t0, t1, t2, t3, left, keep, send, gram):
    half, r = mine.shape[0], mine.shape[1]
    left[pl.ds(pos[2] * half, half)] = mine[...]
    left[pl.ds((1 - pos[2]) * half, half)] = other[...]
    w = jnp.zeros((gate.shape[0], r), F32)
    c = jnp.zeros((r, r), F32)
    for j, stack in enumerate((t0, t1, t2, t3)):
        for k in range(SIDE):
            piece = left[column_block(pos, j, k)]
            w = w + mm(stack[k], piece, 1, 1)
            c = c + mm(piece, piece, 1, 1)
    gram[...] = c
    w_hi, w_lo = split_hi_lo(w)
    v = mm(jnp.concatenate([w_hi, w_lo], 1), gate[...], 0, 0)
    v = v[:r] + v[r:]
    low, high = v[:r // 2], v[r // 2:]
    keep[...] = jnp.where(pos[2] == 0, low, high)
    send[...] = jnp.where(pos[2] == 0, high, low)


def cholesky_kernel(gram, left, out, left_n):
    r = gram.shape[0]
    row_id = lax.broadcasted_iota(jnp.int32, (r, 2 * r), 0)
    lane_id = lax.broadcasted_iota(jnp.int32, (r, 2 * r), 1)
    eye = jnp.where(row_id + r == lane_id, 1.0, 0.0).astype(F32)
    a = jnp.concatenate([gram[...], jnp.zeros((r, r), F32)], 1) + eye
    for k in range(r):
        row = a[k:k + 1, :]
        col = a[:, k:k + 1]
        pivot = a[k:k + 1, k:k + 1]
        scale = jnp.where(row_id[:, :1] > k, col / pivot, 0.0)
        a = a - scale * row
    diag = jnp.sum(jnp.where(row_id == lane_id, a, 0.0), axis=1, keepdims=True)
    out[...] = a[:, r:] / jnp.sqrt(diag)
    for s in range(left.shape[0]):
        left_n[s] = jnp.concatenate([left[s], left[s]], 0).T


def residual_kernel(n_dp, pos, mine, other, inv, gate, left_n, turned, gate_q_t, out_hbm, right, out, sems):
    low = jnp.where(pos[2] == 0, mine[...], other[...])
    high = jnp.where(pos[2] == 0, other[...], mine[...])
    v_t = jnp.concatenate([low, high], 0)
    tokens = gate.shape[0]
    r = v_t.shape[0]
    q = mm_exact(inv[...], v_t, 1, 0) * (1.0 / n_dp)
    gate_q_t[...] = q
    hi, lo = split_hi_lo(-mm_exact(inv[...], q, 0, 0))
    right[:tokens] = gate[...]
    right[tokens:tokens + r] = hi
    right[tokens + r:] = lo
    blocks = sems.shape[0]
    slots, cols = turned.shape[0], turned.shape[1]
    each = slots // blocks
    rows = each * cols

    def copy(i):
        at = pl.ds(pl.multiple_of(i * rows, rows), rows)
        return pltpu.make_async_copy(out.at[at], out_hbm.at[at], sems.at[i])

    def step(i, carry):
        for e in range(each):
            s = i * each + e
            both = jnp.concatenate([turned[s], left_n[s]], 1)
            at = pl.ds(pl.multiple_of(s * cols, cols), cols)
            out[at, :] = mm(both, right[...], 1, 0).astype(out.dtype)
        copy(i).start()
        return carry

    lax.fori_loop(0, blocks, step, 0)

    def finish(i, carry):
        copy(i).wait()
        return carry

    lax.fori_loop(0, blocks, finish, 0)


def residual(pos, mine, other, inv, gate, left_n, turned, n_dp, after=()):
    tokens, width = gate.shape
    n, cols, twice = left_n.shape
    d = n * cols
    blocks = 8

    def body(*refs):
        residual_kernel(n_dp, *refs[:7], *refs[7 + len(after):])

    return pl.pallas_call(
        body,
        in_specs=[smem()] + [vmem()] * 6 + [hbm()] * len(after),
        out_specs=[vmem(), hbm()],
        out_shape=[shape(twice // 2, width, dtype=F32), shape(d, width)],
        scratch_shapes=[
            pltpu.VMEM((tokens + twice, width), BF16),
            pltpu.VMEM((d, width), BF16),
            pltpu.SemaphoreType.DMA((blocks,)),
        ],
        compiler_params=pltpu.CompilerParams(vmem_limit_bytes=32 * MIB),
        cost_estimate=pl.CostEstimate(
            flops=2 * d * width * (tokens + twice), bytes_accessed=2 * d * width, transcendentals=0
        ),
    )(pos, mine, other, inv, gate, left_n, turned, *after)


def plane(n_dp, first, shift):
    pairs = []
    for i in range(n_dp):
        along_x = (i % 2 == 0) == first
        for y in range(SIDE):
            for x in range(SIDE):
                to = (y, (x + shift) % SIDE) if along_x else ((y + shift) % SIDE, x)
                n = SIDE * SIDE
                pairs.append((i * n + y * SIDE + x, i * n + to[0] * SIDE + to[1]))
    return pairs


def ring_pairs(n_dp, step):
    pairs = []
    for i in range(n_dp):
        z, core = i // 2, i % 2
        partner = z ^ 1 if core == step else SIDE - 1 - z
        pairs.append((i, partner * 2 + core))
    return pairs


def local(tokens, gate_pre, up_act, grad_hidden, gate_weight, up_weight, q_init):
    n_dp = lax.axis_size("dp")
    me = lax.axis_index("tensor")
    x, y = me % SIDE, me // SIDE
    core = lax.axis_index("dp") % 2
    a, b = jnp.where(core == 0, x, y), jnp.where(core == 0, y, x)
    pos = jnp.stack([a, b, core]).astype(jnp.int32)
    t_tok, width = gate_pre.shape
    r = q_init.shape[1]
    d = gate_weight.shape[0]
    n = SIDE * SIDE
    cols = d // n

    def over_first(a, k):
        return lax.ppermute(a, ("dp", "tensor"), plane(n_dp, True, k))

    def over_second(a, j):
        return lax.ppermute(a, ("dp", "tensor"), plane(n_dp, False, j))

    def over_ring(a, step):
        return lax.ppermute(a, "dp", ring_pairs(n_dp, step))

    def over_core(a):
        return lax.ppermute(a, "dp", [(i, i ^ 1) for i in range(n_dp)])

    shifts = (1, 3, 2)
    act = pltpu.VMEM((t_tok, width), BF16)
    weights = pltpu.VMEM((d, width), BF16)

    def add(one, two, out, after=()):
        return call(add_kernel, out, [one, two], 1, 1, after=after)

    got = {k: over_first(tokens, k) for k in shifts}
    gate, rel, z_t = call(
        gates_kernel,
        [shape(t_tok, width), shape(t_tok, 2 * width), shape(2 * r, t_tok)],
        [(hbm(), gate_pre), (hbm(), up_act), (hbm(), grad_hidden), q_init.T],
        20 * t_tok * width, 8 * t_tok * width,
        scratch=[act, act, act, pltpu.SemaphoreType.DMA((3,))], pos=pos,
    )
    stack0 = call(
        stack_kernel, shape(SIDE, t_tok, cols), [tokens, got[1], got[2], got[3]], 1, t_tok * d,
        after=[rel],
    )
    far = {j: over_second(stack0, j) for j in shifts}
    stacks = [stack0, far[1], far[2], far[3]]

    parts = call(
        partial_kernel,
        [shape(t_tok // SIDE, d, dtype=F32)] + [shape(t_tok // SIDE, d)] * 3,
        [rel, (hbm(), gate_weight), (hbm(), up_weight)],
        4 * t_tok * width * d, 4 * d * width,
        scratch=[weights, weights, pltpu.SemaphoreType.DMA((8, 2))], mib=48, after=[stack0],
    )
    got = {k: over_first(parts[k], k) for k in shifts}

    keep, send = call(
        left_kernel,
        [shape(n // 2, r, cols, dtype=F32), shape(n // 2, r, cols)],
        [z_t, *stacks], 2 * t_tok * d * 2 * r, 2 * t_tok * d,
        scratch=[pltpu.VMEM((n, r, cols), F32)], pos=pos, after=[parts[0]],
    )
    part_left = shape(n // 2, r, cols)
    pair = add(keep, over_core(send), part_left)
    near = over_ring(pair, 0)
    sums = call(
        sum_split_kernel,
        [shape(t_tok // n, d, dtype=F32)] + [shape(t_tok // n, d)] * 3,
        [parts[0], got[1], got[2], got[3]], 4 * t_tok * d, 4 * t_tok * d, after=[pair],
    )
    got = {j: over_second(sums[j], j) for j in shifts}
    pair = add(pair, near, part_left, after=[sums[0]])
    near = over_ring(pair, 1)
    turned = call(
        turn_kernel, shape(n, cols, t_tok), stacks, 4 * MIB, 4 * t_tok * d, pos=pos, after=[pair]
    )
    piece = call(
        sum_kernel, shape(t_tok // n, d), [sums[0], got[1], got[2], got[3]],
        t_tok * d, t_tok * d, after=[turned],
    )
    got = {j: over_second(piece, j) for j in shifts}
    mine = add(pair, near, part_left, after=[piece])
    other = over_core(mine)
    left, keep, send, gram = call(
        right_kernel,
        [shape(n, r, cols)] + [shape(r // 2, width, dtype=F32)] * 2 + [shape(r, r, dtype=F32)],
        [mine, other, gate, *stacks], 2 * t_tok * d * r, 2 * t_tok * d, pos=pos,
    )
    part_right = shape(r // 2, width, dtype=F32)
    pair = add(keep, over_core(send), part_right)
    near = over_ring(pair, 0)
    quarter = call(
        lambda *refs: place_kernel(1, *refs), shape(t_tok // SIDE, d),
        [piece, got[1], got[2], got[3]], 1, t_tok * d, pos=pos, after=[pair],
    )
    got = {k: over_first(quarter, k) for k in shifts}
    pair = add(pair, near, part_right, after=[quarter])
    near = over_ring(pair, 1)
    inv, left_n = call(
        cholesky_kernel, [shape(r, r, dtype=F32), shape(n, cols, 2 * r)], [gram, left],
        10 * MIB, 4 * r * d, after=[pair],
    )
    mine = add(pair, near, part_right, after=[inv])
    other = over_core(mine)
    gate_q_t, error = residual(pos, mine, other, inv, gate, left_n, turned, n_dp)
    grad_input = call(
        lambda *refs: place_kernel(0, *refs), shape(t_tok, d),
        [quarter, got[1], got[2], got[3]], 1, 4 * t_tok * d, pos=pos, after=[gate_q_t],
    )
    return (grad_input, gate_q_t.T, error)


def solution(mesh):
    return jax.shard_map(
        local,
        mesh=mesh,
        in_specs=(
            P("dp", "tensor"),
            P("dp", "tensor"),
            P("dp", "tensor"),
            P("dp", "tensor"),
            P(None, "tensor"),
            P(None, "tensor"),
            P("tensor", None),
        ),
        out_specs=(P("dp", None), P("tensor", None), P("dp", "tensor")),
        check_vma=False,
    )
```

```python
import jax
import jax.numpy as jnp
from jax import lax
from jax.experimental import pallas as pl
from jax.experimental.pallas import tpu as pltpu
from jax.sharding import PartitionSpec as P

F32 = jnp.float32
BF16 = jnp.bfloat16
SIDE = 4
MIB = 1024 * 1024
COST = {
    "gates": 3,
    "stack": 0.1,
    "partial": 7,
    "left": 1,
    "pair0": 0.1,
    "sums": 0.2,
    "pair1": 0.1,
    "mine": 0.1,
    "right": 0.1,
    "pair2": 0.1,
    "cholesky": 0.5,
    "pair3": 0.1,
    "turn": 1,
    "quarter": 0.6,
    "mine2": 0.1,
    "residual": 3.6,
    "rows": 0.5,
    "own": 3,
}


def mm(a, b, ca, cb):
    return lax.dot_general(a, b, (((ca,), (cb,)), ((), ())), preferred_element_type=F32)


def mm_exact(a, b, ca, cb):
    return lax.dot_general(
        a, b, (((ca,), (cb,)), ((), ())),
        precision=lax.Precision.HIGHEST, preferred_element_type=F32,
    )


def split_hi_lo(a):
    hi = a.astype(BF16)
    return hi, (a - hi.astype(F32)).astype(BF16)


def vmem():
    return pl.BlockSpec(memory_space=pltpu.VMEM)


def hbm():
    return pl.BlockSpec(memory_space=pl.ANY)


def smem():
    return pl.BlockSpec(memory_space=pltpu.SMEM)


def cost(name):
    return pl.CostEstimate(flops=int(COST[name] * 10**9), bytes_accessed=0, transcendentals=0)


def call(name, kernel, outs, ins, scratch=(), mib=32, pos=None, after=()):
    lead = 0 if pos is None else 1
    several = isinstance(outs, (list, tuple))

    def body(*refs):
        kernel(*refs[:lead + len(ins)], *refs[lead + len(ins) + len(after):])

    specs = [x[0] if isinstance(x, tuple) else vmem() for x in ins]
    arrays = [x[1] if isinstance(x, tuple) else x for x in ins]
    return pl.pallas_call(
        body,
        out_shape=outs,
        in_specs=[smem()] * lead + specs + [hbm()] * len(after),
        out_specs=[vmem()] * len(outs) if several else vmem(),
        scratch_shapes=list(scratch),
        compiler_params=pltpu.CompilerParams(vmem_limit_bytes=mib * MIB),
        cost_estimate=cost(name),
    )(*([pos] if lead else []), *arrays, *after)


def shape(*dims, dtype=BF16):
    return jax.ShapeDtypeStruct(dims, dtype)


def gates_kernel(pre_hbm, up_hbm, cot_hbm, q_hbm, tok_hbm, gate, rel, z_t, own, pre_v, up_v, cot_v, q_t, sems):
    pairs = ((pre_hbm, pre_v), (cot_hbm, cot_v), (up_hbm, up_v), (q_hbm, q_t), (tok_hbm, own))
    copies = [pltpu.make_async_copy(src, dst, sems.at[n]) for n, (src, dst) in enumerate(pairs)]
    for copy in copies:
        copy.start()
    for copy in copies:
        copy.wait()
    me = lax.axis_index("tensor")
    a = jnp.where(lax.axis_index("dp") % 2 == 0, me % SIDE, me // SIDE)
    tokens, width = pre_v.shape
    rows = tokens // (SIDE * SIDE)
    for k in range(SIDE):
        for j in range(SIDE):
            src = ((a + k) % SIDE) * SIDE + j
            src = pl.ds(pl.multiple_of(src * rows, rows), rows)
            dst = pl.ds((k * SIDE + j) * rows, rows)
            pre = pre_v[src, :].astype(F32)
            cot = cot_v[src, :].astype(F32)
            sig = 1.0 / (1.0 + jnp.exp(-pre))
            rel[dst, width:] = (cot * pre * sig).astype(BF16)
            grad_gate = (
                cot * up_v[src, :].astype(F32) * sig * (1.0 + pre * (1.0 - sig))
            ).astype(BF16)
            rel[dst, :width] = grad_gate
            gate[src, :] = grad_gate
    q_hi, q_lo = split_hi_lo(q_t[...])
    z = mm(jnp.concatenate([q_hi, q_lo], 0), gate[...], 1, 1)
    r = q_t.shape[0]
    z_hi, z_lo = split_hi_lo(z[:r] + z[r:])
    z_t[:r] = z_hi
    z_t[r:] = z_lo


def partial_kernel(rel, gate_hbm, up_hbm, o0, o1, o2, o3, gate_v, up_v, sems):
    blocks = sems.shape[0]
    d, width = gate_v.shape
    block = d // blocks

    def copies(i):
        at = pl.ds(pl.multiple_of(i * block, block), block)
        return (
            pltpu.make_async_copy(gate_hbm.at[at], gate_v.at[at], sems.at[i, 0]),
            pltpu.make_async_copy(up_hbm.at[at], up_v.at[at], sems.at[i, 1]),
        )

    for i in range(blocks):
        for copy in copies(i):
            copy.start()

    def step(i, carry):
        for copy in copies(i):
            copy.wait()
        at = pl.ds(pl.multiple_of(i * block, block), block)
        acc = mm(rel[:, :width], gate_v[at, :], 1, 1) + mm(rel[:, width:], up_v[at, :], 1, 1)
        rows = acc.shape[0] // SIDE
        for k, out in enumerate((o0, o1, o2, o3)):
            out[:, at] = acc[k * rows:(k + 1) * rows].astype(out.dtype)
        return carry

    lax.fori_loop(0, blocks, step, 0)


def stack_kernel(own, a, b, c, out):
    for k, block in enumerate((own, a, b, c)):
        out[k] = block[...]


def sum_kernel(own, a, b, c, out):
    total = (own[...].astype(F32) + b[...].astype(F32)) + (a[...].astype(F32) + c[...].astype(F32))
    out[...] = total.astype(out.dtype)


def copy_kernel(one, out):
    out[...] = one[...]


def add_kernel(one, two, out):
    out[...] = (one[...].astype(F32) + two[...].astype(F32)).astype(out.dtype)


def column_block(pos, j, k):
    first, second = (pos[0] + SIDE - k) % SIDE, (pos[1] + SIDE - j) % SIDE
    return jnp.where(pos[2] == 0, second * SIDE + first, first * SIDE + second)


def place_rows(steps, pos, blocks, out, sems):
    rows = blocks[0].shape[0]
    copies = []
    for i, k in enumerate(steps):
        at = (pos[0] + SIDE - k) % SIDE
        at = pl.ds(pl.multiple_of(at * rows, rows), rows)
        copies.append(pltpu.make_async_copy(blocks[i], out.at[at], sems.at[i]))
        copies[-1].start()
    return copies


def put_rows(steps, pos, blocks, so_far):
    n = len(blocks)

    def kernel(pos, *refs):
        for copy in place_rows(steps, pos, refs[:n], refs[n + 1], refs[n + 2]):
            copy.wait()

    return pl.pallas_call(
        kernel,
        in_specs=[smem()] + [vmem()] * n + [hbm()],
        out_specs=hbm(),
        out_shape=shape(*so_far.shape),
        scratch_shapes=[pltpu.SemaphoreType.DMA((n,))],
        input_output_aliases={1 + n: 0},
        compiler_params=pltpu.CompilerParams(vmem_limit_bytes=MIB),
        cost_estimate=cost("rows"),
    )(pos, *blocks, so_far)


def left_kernel(pos, z_t, t0, t1, t2, t3, keep, send, whole):
    half, r = keep.shape[0], keep.shape[1]
    for j, stack in enumerate((t0, t1, t2, t3)):
        for k in range(SIDE):
            part = mm(z_t[...], stack[k], 1, 0)
            whole[column_block(pos, j, k)] = part[:r] + part[r:]
    keep[...] = whole[pl.ds(pos[2] * half, half)]
    send[...] = whole[pl.ds((1 - pos[2]) * half, half)].astype(send.dtype)


def turn_kernel(pos, t0, t1, t2, t3, out):
    for j, stack in enumerate((t0, t1, t2, t3)):
        for k in range(SIDE):
            out[column_block(pos, j, k)] = stack[k].T


def right_kernel(pos, mine, other, gate, t0, t1, t2, t3, left, keep, send, gram):
    half, r = mine.shape[0], mine.shape[1]
    left[pl.ds(pos[2] * half, half)] = mine[...]
    left[pl.ds((1 - pos[2]) * half, half)] = other[...]
    w = jnp.zeros((gate.shape[0], r), F32)
    c = jnp.zeros((r, r), F32)
    for j, stack in enumerate((t0, t1, t2, t3)):
        for k in range(SIDE):
            piece = left[column_block(pos, j, k)]
            w = w + mm(stack[k], piece, 1, 1)
            c = c + mm(piece, piece, 1, 1)
    gram[...] = c
    w_hi, w_lo = split_hi_lo(w)
    v = mm(jnp.concatenate([w_hi, w_lo], 1), gate[...], 0, 0)
    v = v[:r] + v[r:]
    low, high = v[:r // 2], v[r // 2:]
    keep[...] = jnp.where(pos[2] == 0, low, high)
    send[...] = jnp.where(pos[2] == 0, high, low)


def cholesky_kernel(gram, left, out, left_n):
    r = gram.shape[0]
    row_id = lax.broadcasted_iota(jnp.int32, (r, 2 * r), 0)
    lane_id = lax.broadcasted_iota(jnp.int32, (r, 2 * r), 1)
    eye = jnp.where(row_id + r == lane_id, 1.0, 0.0).astype(F32)
    a = jnp.concatenate([gram[...], jnp.zeros((r, r), F32)], 1) + eye
    for k in range(r):
        row = a[k:k + 1, :]
        col = a[:, k:k + 1]
        pivot = a[k:k + 1, k:k + 1]
        scale = jnp.where(row_id[:, :1] > k, col / pivot, 0.0)
        a = a - scale * row
    diag = jnp.sum(jnp.where(row_id == lane_id, a, 0.0), axis=1, keepdims=True)
    out[...] = a[:, r:] / jnp.sqrt(diag)
    for s in range(left.shape[0]):
        left_n[s] = jnp.concatenate([left[s], left[s]], 0).T


def residual_kernel(
    n_dp, pos, mine, other, inv, gate, left_n, turned, quarter,
    gate_q_t, out_hbm, grad_input, right, out, sems, row_sems,
):
    own_rows = place_rows((0,), pos, (quarter,), grad_input, row_sems)
    low = jnp.where(pos[2] == 0, mine[...], other[...])
    high = jnp.where(pos[2] == 0, other[...], mine[...])
    v_t = jnp.concatenate([low, high], 0)
    r = v_t.shape[0]
    q = mm_exact(inv[...], v_t, 1, 0) * (1.0 / n_dp)
    gate_q_t[...] = q
    hi, lo = split_hi_lo(-mm_exact(inv[...], q, 0, 0))
    right[:r] = hi
    right[r:] = lo
    blocks = sems.shape[0]
    slots, cols = turned.shape[0], turned.shape[1]
    each = slots // blocks
    rows = each * cols
    copies = []
    for i in range(blocks):
        for s in range(i * each, (i + 1) * each):
            out[s * cols:(s + 1) * cols, :] = (
                mm(turned[s], gate[...], 1, 0) + mm(left_n[s], right[...], 1, 0)
            ).astype(out.dtype)
        at = pl.ds(i * rows, rows)
        copies.append(pltpu.make_async_copy(out.at[at], out_hbm.at[at], sems.at[i]))
        copies[-1].start()
    for copy in copies + own_rows:
        copy.wait()


def residual(pos, mine, other, inv, gate, left_n, turned, quarter, n_dp):
    tokens, width = gate.shape
    n, cols, twice = left_n.shape
    d = n * cols
    blocks = 8
    return pl.pallas_call(
        lambda *refs: residual_kernel(n_dp, *refs),
        in_specs=[smem()] + [vmem()] * 7,
        out_specs=[vmem(), hbm(), hbm()],
        out_shape=[shape(twice // 2, width, dtype=F32), shape(d, width), shape(tokens, d)],
        scratch_shapes=[
            pltpu.VMEM((twice, width), BF16),
            pltpu.VMEM((d, width), BF16),
            pltpu.SemaphoreType.DMA((blocks,)),
            pltpu.SemaphoreType.DMA((1,)),
        ],
        compiler_params=pltpu.CompilerParams(vmem_limit_bytes=32 * MIB),
        cost_estimate=cost("residual"),
    )(pos, mine, other, inv, gate, left_n, turned, quarter)


def plane(n_dp, first, shift):
    pairs = []
    for i in range(n_dp):
        along_x = (i % 2 == 0) == first
        for y in range(SIDE):
            for x in range(SIDE):
                to = (y, (x + shift) % SIDE) if along_x else ((y + shift) % SIDE, x)
                n = SIDE * SIDE
                pairs.append((i * n + y * SIDE + x, i * n + to[0] * SIDE + to[1]))
    return pairs


def ring_pairs(n_dp, step):
    pairs = []
    for i in range(n_dp):
        z, core = i // 2, i % 2
        partner = z ^ 1 if core == step else SIDE - 1 - z
        pairs.append((i, partner * 2 + core))
    return pairs


def local(tokens, gate_pre, up_act, grad_hidden, gate_weight, up_weight, q_init):
    n_dp = lax.axis_size("dp")
    me = lax.axis_index("tensor")
    x, y = me % SIDE, me // SIDE
    core = lax.axis_index("dp") % 2
    a, b = jnp.where(core == 0, x, y), jnp.where(core == 0, y, x)
    pos = jnp.stack([a, b, core]).astype(jnp.int32)
    t_tok, width = gate_pre.shape
    r = q_init.shape[1]
    d = gate_weight.shape[0]
    n = SIDE * SIDE
    cols = d // n

    def over_first(a, k):
        return lax.ppermute(a, ("dp", "tensor"), plane(n_dp, True, k))

    def over_second(a, j):
        return lax.ppermute(a, ("dp", "tensor"), plane(n_dp, False, j))

    def over_ring(a, step):
        return lax.ppermute(a, "dp", ring_pairs(n_dp, step))

    def over_core(a):
        return lax.ppermute(a, "dp", [(i, i ^ 1) for i in range(n_dp)])

    shifts = (1, 3, 2)
    act = pltpu.VMEM((t_tok, width), BF16)
    weights = pltpu.VMEM((d, width), BF16)

    def add(name, one, two, out, after=()):
        return call(name, add_kernel, out, [one, two], after=after)

    got = {k: over_first(tokens, k) for k in shifts}
    gate, rel, z_t, own = call(
        "gates", gates_kernel,
        [shape(t_tok, width), shape(t_tok, 2 * width), shape(2 * r, t_tok), shape(t_tok, cols)],
        [(hbm(), a) for a in (gate_pre, up_act, grad_hidden, q_init.T, tokens)],
        scratch=[act, act, act, pltpu.VMEM((r, width), F32), pltpu.SemaphoreType.DMA((5,))],
        mib=60,
    )
    own = call("own", copy_kernel, shape(t_tok, cols), [own])
    stack0 = call(
        "stack", stack_kernel, shape(SIDE, t_tok, cols), [own, got[1], got[2], got[3]]
    )
    far = {j: over_second(stack0, j) for j in shifts}
    stacks = [stack0, far[1], far[2], far[3]]

    parts = call(
        "partial", partial_kernel,
        [shape(t_tok // SIDE, d, dtype=F32)] + [shape(t_tok // SIDE, d)] * 3,
        [rel, (hbm(), gate_weight), (hbm(), up_weight)],
        scratch=[weights, weights, pltpu.SemaphoreType.DMA((8, 2))], mib=48, after=[stack0],
    )
    got = {k: over_first(parts[k], k) for k in shifts}

    part_left = shape(n // 2, r, cols)
    keep, send = call(
        "left", left_kernel, [shape(n // 2, r, cols, dtype=F32), part_left], [z_t, *stacks],
        scratch=[pltpu.VMEM((n, r, cols), F32)], pos=pos, after=[parts[0]],
    )
    pair = add("pair0", keep, over_core(send), part_left)
    near = over_ring(pair, 0)
    turned = call("turn", turn_kernel, shape(n, cols, t_tok), stacks, pos=pos, after=[pair])
    sums = call(
        "sums", sum_kernel, shape(t_tok // SIDE, d), [parts[0], got[1], got[2], got[3]],
        after=[turned],
    )
    got = {j: over_second(sums, j) for j in shifts}
    pair = add("pair1", pair, near, part_left, after=[sums])
    near = over_ring(pair, 1)
    mine = add("mine", pair, near, part_left)
    other = over_core(mine)
    left, keep, send, gram = call(
        "right", right_kernel,
        [shape(n, r, cols)] + [shape(r // 2, width, dtype=F32)] * 2 + [shape(r, r, dtype=F32)],
        [mine, other, gate, *stacks], pos=pos,
    )

    part_right = shape(r // 2, width, dtype=F32)
    pair = add("pair2", keep, over_core(send), part_right)
    near = over_ring(pair, 0)
    inv, left_n = call(
        "cholesky", cholesky_kernel, [shape(r, r, dtype=F32), shape(n, cols, 2 * r)], [gram, left],
        after=[pair],
    )
    pair = add("pair3", pair, near, part_right, after=[inv])
    near = over_ring(pair, 1)
    quarter = call(
        "quarter", sum_kernel, shape(t_tok // SIDE, d), [sums, got[1], got[2], got[3]],
        after=[pair],
    )
    got = {k: over_first(quarter, k) for k in shifts}
    mine = add("mine2", pair, near, part_right, after=[quarter])
    other = over_core(mine)
    gate_q_t, error, rows = residual(pos, mine, other, inv, gate, left_n, turned, quarter, n_dp)
    grad_input = put_rows((2, 1, 3), pos, [got[k] for k in (2, 1, 3)], rows)
    return (grad_input, gate_q_t.T, error)


def solution(mesh):
    return jax.shard_map(
        local,
        mesh=mesh,
        in_specs=(
            P("dp", "tensor"),
            P("dp", "tensor"),
            P("dp", "tensor"),
            P("dp", "tensor"),
            P(None, "tensor"),
            P(None, "tensor"),
            P("tensor", None),
        ),
        out_specs=(P("dp", None), P("tensor", None), P("dp", "tensor")),
        check_vma=False,
    )
```

```python
import jax
import jax.numpy as jnp
from jax import lax
from jax.experimental import pallas as pl
from jax.experimental.pallas import tpu as pltpu
from jax.sharding import PartitionSpec as P

F32 = jnp.float32
BF16 = jnp.bfloat16
SIDE = 4
MIB = 1024 * 1024
COST = {
    "gates": 3,
    "stack": 0.1,
    "partial": 7,
    "left": 1,
    "pair0": 0.1,
    "sums": 0.2,
    "pair1": 0.1,
    "mine": 0.1,
    "right": 0.1,
    "pair2": 0.1,
    "cholesky": 0.5,
    "pair3": 0.1,
    "turn": 1,
    "quarter": 0.6,
    "mine2": 0.1,
    "residual": 3.6,
    "rows": 0.5,
    "own": 3,
}


def mm(a, b, ca, cb):
    return lax.dot_general(a, b, (((ca,), (cb,)), ((), ())), preferred_element_type=F32)


def mm_exact(a, b, ca, cb):
    return lax.dot_general(
        a, b, (((ca,), (cb,)), ((), ())),
        precision=lax.Precision.HIGHEST, preferred_element_type=F32,
    )


def split_hi_lo(a):
    hi = a.astype(BF16)
    return hi, (a - hi.astype(F32)).astype(BF16)


def vmem():
    return pl.BlockSpec(memory_space=pltpu.VMEM)


def hbm():
    return pl.BlockSpec(memory_space=pl.ANY)


def smem():
    return pl.BlockSpec(memory_space=pltpu.SMEM)


def cost(name):
    return pl.CostEstimate(flops=int(COST[name] * 10**9), bytes_accessed=0, transcendentals=0)


def call(name, kernel, outs, ins, scratch=(), mib=32, pos=None, after=()):
    lead = 0 if pos is None else 1
    several = isinstance(outs, (list, tuple))

    def body(*refs):
        kernel(*refs[:lead + len(ins)], *refs[lead + len(ins) + len(after):])

    specs = [x[0] if isinstance(x, tuple) else vmem() for x in ins]
    arrays = [x[1] if isinstance(x, tuple) else x for x in ins]
    return pl.pallas_call(
        body,
        out_shape=outs,
        in_specs=[smem()] * lead + specs + [hbm()] * len(after),
        out_specs=[vmem()] * len(outs) if several else vmem(),
        scratch_shapes=list(scratch),
        compiler_params=pltpu.CompilerParams(vmem_limit_bytes=mib * MIB),
        cost_estimate=cost(name),
    )(*([pos] if lead else []), *arrays, *after)


def shape(*dims, dtype=BF16):
    return jax.ShapeDtypeStruct(dims, dtype)


def gates_kernel(pre_hbm, up_hbm, cot_hbm, q_hbm, tok_hbm, gate, rel, z_t, own, pre_v, up_v, cot_v, q_t, sems):
    pairs = ((pre_hbm, pre_v), (cot_hbm, cot_v), (up_hbm, up_v), (q_hbm, q_t), (tok_hbm, own))
    copies = [pltpu.make_async_copy(src, dst, sems.at[n]) for n, (src, dst) in enumerate(pairs)]
    for copy in copies:
        copy.start()
    for copy in copies:
        copy.wait()
    me = lax.axis_index("tensor")
    a = jnp.where(lax.axis_index("dp") % 2 == 0, me % SIDE, me // SIDE)
    tokens, width = pre_v.shape
    rows = tokens // (SIDE * SIDE)
    for k in range(SIDE):
        for j in range(SIDE):
            src = ((a + k) % SIDE) * SIDE + j
            src = pl.ds(pl.multiple_of(src * rows, rows), rows)
            dst = pl.ds((k * SIDE + j) * rows, rows)
            pre = pre_v[src, :].astype(F32)
            cot = cot_v[src, :].astype(F32)
            sig = 1.0 / (1.0 + jnp.exp(-pre))
            rel[dst, width:] = (cot * pre * sig).astype(BF16)
            grad_gate = (
                cot * up_v[src, :].astype(F32) * sig * (1.0 + pre * (1.0 - sig))
            ).astype(BF16)
            rel[dst, :width] = grad_gate
            gate[src, :] = grad_gate
    q_hi, q_lo = split_hi_lo(q_t[...])
    z = mm(jnp.concatenate([q_hi, q_lo], 0), gate[...], 1, 1)
    r = q_t.shape[0]
    z_hi, z_lo = split_hi_lo(z[:r] + z[r:])
    z_t[:r] = z_hi
    z_t[r:] = z_lo


def partial_kernel(rel, gate_hbm, up_hbm, o0, o1, o2, o3, gate_v, up_v, sems):
    blocks = sems.shape[0]
    d, width = gate_v.shape
    block = d // blocks

    def copies(i):
        at = pl.ds(pl.multiple_of(i * block, block), block)
        return (
            pltpu.make_async_copy(gate_hbm.at[at], gate_v.at[at], sems.at[i, 0]),
            pltpu.make_async_copy(up_hbm.at[at], up_v.at[at], sems.at[i, 1]),
        )

    for i in range(blocks):
        for copy in copies(i):
            copy.start()

    def step(i, carry):
        for copy in copies(i):
            copy.wait()
        at = pl.ds(pl.multiple_of(i * block, block), block)
        acc = mm(rel[:, :width], gate_v[at, :], 1, 1) + mm(rel[:, width:], up_v[at, :], 1, 1)
        rows = acc.shape[0] // SIDE
        for k, out in enumerate((o0, o1, o2, o3)):
            out[:, at] = acc[k * rows:(k + 1) * rows].astype(out.dtype)
        return carry

    lax.fori_loop(0, blocks, step, 0)


def stack_kernel(own, a, b, c, out):
    for k, block in enumerate((own, a, b, c)):
        out[k] = block[...]


def sum_kernel(own, a, c, b, out):
    total = (own[...].astype(F32) + b[...].astype(F32)) + (a[...].astype(F32) + c[...].astype(F32))
    out[...] = total.astype(out.dtype)


def copy_kernel(one, out):
    out[...] = one[...]


def add_kernel(one, two, out):
    out[...] = (one[...].astype(F32) + two[...].astype(F32)).astype(out.dtype)


def column_block(pos, j, k):
    first, second = (pos[0] + SIDE - k) % SIDE, (pos[1] + SIDE - j) % SIDE
    return jnp.where(pos[2] == 0, second * SIDE + first, first * SIDE + second)


def place_rows(steps, pos, blocks, out, sems):
    rows = blocks[0].shape[0]
    copies = []
    for i, k in enumerate(steps):
        at = (pos[0] + SIDE - k) % SIDE
        at = pl.ds(pl.multiple_of(at * rows, rows), rows)
        copies.append(pltpu.make_async_copy(blocks[i], out.at[at], sems.at[i]))
        copies[-1].start()
    return copies


def put_rows(steps, pos, blocks, so_far):
    n = len(blocks)

    def kernel(pos, *refs):
        for copy in place_rows(steps, pos, refs[:n], refs[n + 1], refs[n + 2]):
            copy.wait()

    return pl.pallas_call(
        kernel,
        in_specs=[smem()] + [vmem()] * n + [hbm()],
        out_specs=hbm(),
        out_shape=shape(*so_far.shape),
        scratch_shapes=[pltpu.SemaphoreType.DMA((n,))],
        input_output_aliases={1 + n: 0},
        compiler_params=pltpu.CompilerParams(vmem_limit_bytes=MIB),
        cost_estimate=cost("rows"),
    )(pos, *blocks, so_far)


def left_kernel(pos, z_t, t0, t1, t3, t2, keep, send, whole):
    half, r = keep.shape[0], keep.shape[1]
    for j, stack in enumerate((t0, t1, t2, t3)):
        for k in range(SIDE):
            part = mm(z_t[...], stack[k], 1, 0)
            whole[column_block(pos, j, k)] = part[:r] + part[r:]
    keep[...] = whole[pl.ds(pos[2] * half, half)]
    send[...] = whole[pl.ds((1 - pos[2]) * half, half)].astype(send.dtype)


def turn_kernel(pos, t0, t1, t3, t2, out):
    for j, stack in enumerate((t0, t1, t2, t3)):
        for k in range(SIDE):
            out[column_block(pos, j, k)] = stack[k].T


def right_kernel(pos, mine, other, gate, t0, t1, t3, t2, left, keep, send, gram):
    half, r = mine.shape[0], mine.shape[1]
    left[pl.ds(pos[2] * half, half)] = mine[...]
    left[pl.ds((1 - pos[2]) * half, half)] = other[...]
    w = jnp.zeros((gate.shape[0], r), F32)
    c = jnp.zeros((r, r), F32)
    for j, stack in enumerate((t0, t1, t2, t3)):
        for k in range(SIDE):
            piece = left[column_block(pos, j, k)]
            w = w + mm(stack[k], piece, 1, 1)
            c = c + mm(piece, piece, 1, 1)
    gram[...] = c
    w_hi, w_lo = split_hi_lo(w)
    v = mm(jnp.concatenate([w_hi, w_lo], 1), gate[...], 0, 0)
    v = v[:r] + v[r:]
    low, high = v[:r // 2], v[r // 2:]
    keep[...] = jnp.where(pos[2] == 0, low, high)
    send[...] = jnp.where(pos[2] == 0, high, low)


def cholesky_kernel(gram, left, out, left_n):
    r = gram.shape[0]
    row_id = lax.broadcasted_iota(jnp.int32, (r, 2 * r), 0)
    lane_id = lax.broadcasted_iota(jnp.int32, (r, 2 * r), 1)
    eye = jnp.where(row_id + r == lane_id, 1.0, 0.0).astype(F32)
    a = jnp.concatenate([gram[...], jnp.zeros((r, r), F32)], 1) + eye
    for k in range(r):
        row = a[k:k + 1, :]
        col = a[:, k:k + 1]
        pivot = a[k:k + 1, k:k + 1]
        scale = jnp.where(row_id[:, :1] > k, col / pivot, 0.0)
        a = a - scale * row
    diag = jnp.sum(jnp.where(row_id == lane_id, a, 0.0), axis=1, keepdims=True)
    out[...] = a[:, r:] / jnp.sqrt(diag)
    for s in range(left.shape[0]):
        left_n[s] = jnp.concatenate([left[s], left[s]], 0).T


def residual_kernel(
    n_dp, pos, mine, other, inv, gate, left_n, turned, quarter,
    gate_q_t, out_hbm, grad_input, right, out, sems, row_sems,
):
    own_rows = place_rows((0,), pos, (quarter,), grad_input, row_sems)
    low = jnp.where(pos[2] == 0, mine[...], other[...])
    high = jnp.where(pos[2] == 0, other[...], mine[...])
    v_t = jnp.concatenate([low, high], 0)
    r = v_t.shape[0]
    q = mm_exact(inv[...], v_t, 1, 0) * (1.0 / n_dp)
    gate_q_t[...] = q
    hi, lo = split_hi_lo(-mm_exact(inv[...], q, 0, 0))
    right[:r] = hi
    right[r:] = lo
    blocks = sems.shape[0]
    slots, cols = turned.shape[0], turned.shape[1]
    each = slots // blocks
    rows = each * cols
    copies = []
    for i in range(blocks):
        for s in range(i * each, (i + 1) * each):
            out[s * cols:(s + 1) * cols, :] = (
                mm(turned[s], gate[...], 1, 0) + mm(left_n[s], right[...], 1, 0)
            ).astype(out.dtype)
        at = pl.ds(i * rows, rows)
        copies.append(pltpu.make_async_copy(out.at[at], out_hbm.at[at], sems.at[i]))
        copies[-1].start()
    for copy in copies + own_rows:
        copy.wait()


def residual(pos, mine, other, inv, gate, left_n, turned, quarter, n_dp):
    tokens, width = gate.shape
    n, cols, twice = left_n.shape
    d = n * cols
    blocks = 8
    return pl.pallas_call(
        lambda *refs: residual_kernel(n_dp, *refs),
        in_specs=[smem()] + [vmem()] * 7,
        out_specs=[vmem(), hbm(), hbm()],
        out_shape=[shape(twice // 2, width, dtype=F32), shape(d, width), shape(tokens, d)],
        scratch_shapes=[
            pltpu.VMEM((twice, width), BF16),
            pltpu.VMEM((d, width), BF16),
            pltpu.SemaphoreType.DMA((blocks,)),
            pltpu.SemaphoreType.DMA((1,)),
        ],
        compiler_params=pltpu.CompilerParams(vmem_limit_bytes=32 * MIB),
        cost_estimate=cost("residual"),
    )(pos, mine, other, inv, gate, left_n, turned, quarter)


def plane(n_dp, first, shift):
    pairs = []
    for i in range(n_dp):
        along_x = (i % 2 == 0) == first
        for y in range(SIDE):
            for x in range(SIDE):
                to = (y, (x + shift) % SIDE) if along_x else ((y + shift) % SIDE, x)
                n = SIDE * SIDE
                pairs.append((i * n + y * SIDE + x, i * n + to[0] * SIDE + to[1]))
    return pairs


def ring_pairs(n_dp, step):
    pairs = []
    for i in range(n_dp):
        z, core = i // 2, i % 2
        partner = z ^ 1 if core == step else SIDE - 1 - z
        pairs.append((i, partner * 2 + core))
    return pairs


def local(tokens, gate_pre, up_act, grad_hidden, gate_weight, up_weight, q_init):
    n_dp = lax.axis_size("dp")
    me = lax.axis_index("tensor")
    x, y = me % SIDE, me // SIDE
    core = lax.axis_index("dp") % 2
    a, b = jnp.where(core == 0, x, y), jnp.where(core == 0, y, x)
    pos = jnp.stack([a, b, core]).astype(jnp.int32)
    t_tok, width = gate_pre.shape
    r = q_init.shape[1]
    d = gate_weight.shape[0]
    n = SIDE * SIDE
    cols = d // n

    def over_first(a, k):
        return lax.ppermute(a, ("dp", "tensor"), plane(n_dp, True, k))

    def over_second(a, j):
        return lax.ppermute(a, ("dp", "tensor"), plane(n_dp, False, j))

    def over_ring(a, step):
        return lax.ppermute(a, "dp", ring_pairs(n_dp, step))

    def over_core(a):
        return lax.ppermute(a, "dp", [(i, i ^ 1) for i in range(n_dp)])

    shifts = (1, 3, 2)
    act = pltpu.VMEM((t_tok, width), BF16)
    weights = pltpu.VMEM((d, width), BF16)

    def add(name, one, two, out, after=()):
        return call(name, add_kernel, out, [one, two], after=after)

    got = {k: over_first(tokens, k) for k in shifts}
    gate, rel, z_t, own = call(
        "gates", gates_kernel,
        [shape(t_tok, width), shape(t_tok, 2 * width), shape(2 * r, t_tok), shape(t_tok, cols)],
        [(hbm(), a) for a in (gate_pre, up_act, grad_hidden, q_init.T, tokens)],
        scratch=[act, act, act, pltpu.VMEM((r, width), F32), pltpu.SemaphoreType.DMA((5,))],
        mib=60,
    )
    own = call("own", copy_kernel, shape(t_tok, cols), [own])
    stack0 = call(
        "stack", stack_kernel, shape(SIDE, t_tok, cols), [own, got[1], got[2], got[3]]
    )
    far = {j: over_second(stack0, j) for j in shifts}
    stacks = [stack0, far[1], far[3], far[2]]

    parts = call(
        "partial", partial_kernel,
        [shape(t_tok // SIDE, d, dtype=F32)] + [shape(t_tok // SIDE, d)] * 3,
        [rel, (hbm(), gate_weight), (hbm(), up_weight)],
        scratch=[weights, weights, pltpu.SemaphoreType.DMA((8, 2))], mib=48, after=[stack0],
    )
    got = {k: over_first(parts[k], k) for k in shifts}

    part_left = shape(n // 2, r, cols)
    keep, send = call(
        "left", left_kernel, [shape(n // 2, r, cols, dtype=F32), part_left],
        [z_t, *stacks],
        scratch=[pltpu.VMEM((n, r, cols), F32)], pos=pos, after=[parts[0]],
    )
    pair = add("pair0", keep, over_core(send), part_left)
    near = over_ring(pair, 0)
    turned = call("turn", turn_kernel, shape(n, cols, t_tok), stacks, pos=pos, after=[pair])
    sums = call(
        "sums", sum_kernel, shape(t_tok // SIDE, d), [parts[0], got[1], got[3], got[2]],
        after=[turned],
    )
    got = {j: over_second(sums, j) for j in shifts}
    pair = add("pair1", pair, near, part_left, after=[sums])
    near = over_ring(pair, 1)
    mine = add("mine", pair, near, part_left)
    other = over_core(mine)
    left, keep, send, gram = call(
        "right", right_kernel,
        [shape(n, r, cols)] + [shape(r // 2, width, dtype=F32)] * 2 + [shape(r, r, dtype=F32)],
        [mine, other, gate, *stacks], pos=pos,
    )

    part_right = shape(r // 2, width, dtype=F32)
    pair = add("pair2", keep, over_core(send), part_right)
    near = over_ring(pair, 0)
    inv, left_n = call(
        "cholesky", cholesky_kernel, [shape(r, r, dtype=F32), shape(n, cols, 2 * r)], [gram, left],
        after=[pair],
    )
    pair = add("pair3", pair, near, part_right, after=[inv])
    near = over_ring(pair, 1)
    quarter = call(
        "quarter", sum_kernel, shape(t_tok // SIDE, d), [sums, got[1], got[3], got[2]],
        after=[pair],
    )
    got = {k: over_first(quarter, k) for k in shifts}
    mine = add("mine2", pair, near, part_right, after=[quarter])
    other = over_core(mine)
    gate_q_t, error, rows = residual(pos, mine, other, inv, gate, left_n, turned, quarter, n_dp)
    grad_input = put_rows((2, 1, 3), pos, [got[k] for k in (2, 1, 3)], rows)
    return (grad_input, gate_q_t.T, error)


def solution(mesh):
    return jax.shard_map(
        local,
        mesh=mesh,
        in_specs=(
            P("dp", "tensor"),
            P("dp", "tensor"),
            P("dp", "tensor"),
            P("dp", "tensor"),
            P(None, "tensor"),
            P(None, "tensor"),
            P("tensor", None),
        ),
        out_specs=(P("dp", None), P("tensor", None), P("dp", "tensor")),
        check_vma=False,
    )
```

```python
import jax
import jax.numpy as jnp
from jax import lax
from jax.experimental import pallas as pl
from jax.experimental.pallas import tpu as pltpu
from jax.sharding import PartitionSpec as P

F32 = jnp.float32
BF16 = jnp.bfloat16
SIDE = 4
MIB = 1024 * 1024
COST = {
    "gates": 3,
    "stack": 0.1,
    "partial": 7,
    "left": 1,
    "pair0": 0.1,
    "sums": 0.2,
    "pair1": 0.1,
    "mine": 0.1,
    "right": 0.1,
    "pair2": 0.1,
    "cholesky": 0.3,
    "pair3": 0.1,
    "turn": 1,
    "quarter": 0.6,
    "mine2": 0.1,
    "residual": 3.6,
    "rows": 0.5,
    "own": 3,
    "inverse": 0.2,
}


def mm(a, b, ca, cb):
    return lax.dot_general(a, b, (((ca,), (cb,)), ((), ())), preferred_element_type=F32)


def mm_exact(a, b, ca, cb):
    return lax.dot_general(
        a, b, (((ca,), (cb,)), ((), ())),
        precision=lax.Precision.HIGHEST, preferred_element_type=F32,
    )


def split_hi_lo(a):
    hi = a.astype(BF16)
    return hi, (a - hi.astype(F32)).astype(BF16)


def vmem():
    return pl.BlockSpec(memory_space=pltpu.VMEM)


def hbm():
    return pl.BlockSpec(memory_space=pl.ANY)


def smem():
    return pl.BlockSpec(memory_space=pltpu.SMEM)


def cost(name):
    return pl.CostEstimate(flops=int(COST[name] * 10**9), bytes_accessed=0, transcendentals=0)


def call(name, kernel, outs, ins, scratch=(), mib=32, pos=None, after=()):
    lead = 0 if pos is None else 1
    several = isinstance(outs, (list, tuple))

    def body(*refs):
        kernel(*refs[:lead + len(ins)], *refs[lead + len(ins) + len(after):])

    specs = [x[0] if isinstance(x, tuple) else vmem() for x in ins]
    arrays = [x[1] if isinstance(x, tuple) else x for x in ins]
    return pl.pallas_call(
        body,
        out_shape=outs,
        in_specs=[smem()] * lead + specs + [hbm()] * len(after),
        out_specs=[vmem()] * len(outs) if several else vmem(),
        scratch_shapes=list(scratch),
        compiler_params=pltpu.CompilerParams(vmem_limit_bytes=mib * MIB),
        cost_estimate=cost(name),
    )(*([pos] if lead else []), *arrays, *after)


def shape(*dims, dtype=BF16):
    return jax.ShapeDtypeStruct(dims, dtype)


def gates_kernel(pre_hbm, up_hbm, cot_hbm, q_hbm, tok_hbm, gate, rel, z_t, own, pre_v, up_v, cot_v, q_t, sems):
    pairs = ((pre_hbm, pre_v), (cot_hbm, cot_v), (up_hbm, up_v), (q_hbm, q_t), (tok_hbm, own))
    copies = [pltpu.make_async_copy(src, dst, sems.at[n]) for n, (src, dst) in enumerate(pairs)]
    for copy in copies:
        copy.start()
    for copy in copies:
        copy.wait()
    me = lax.axis_index("tensor")
    a = jnp.where(lax.axis_index("dp") % 2 == 0, me % SIDE, me // SIDE)
    tokens, width = pre_v.shape
    rows = tokens // (SIDE * SIDE)
    for k in range(SIDE):
        for j in range(SIDE):
            src = ((a + k) % SIDE) * SIDE + j
            src = pl.ds(pl.multiple_of(src * rows, rows), rows)
            dst = pl.ds((k * SIDE + j) * rows, rows)
            pre = pre_v[src, :].astype(F32)
            cot = cot_v[src, :].astype(F32)
            sig = 1.0 / (1.0 + jnp.exp(-pre))
            rel[dst, width:] = (cot * pre * sig).astype(BF16)
            grad_gate = (
                cot * up_v[src, :].astype(F32) * sig * (1.0 + pre * (1.0 - sig))
            ).astype(BF16)
            rel[dst, :width] = grad_gate
            gate[src, :] = grad_gate
    q_hi, q_lo = split_hi_lo(q_t[...])
    z = mm(jnp.concatenate([q_hi, q_lo], 0), gate[...], 1, 1)
    r = q_t.shape[0]
    z_hi, z_lo = split_hi_lo(z[:r] + z[r:])
    z_t[:r] = z_hi
    z_t[r:] = z_lo


def partial_kernel(rel, gate_hbm, up_hbm, o0, o1, o2, o3, gate_v, up_v, sems):
    blocks = sems.shape[0]
    d, width = gate_v.shape
    block = d // blocks

    def copies(i):
        at = pl.ds(pl.multiple_of(i * block, block), block)
        return (
            pltpu.make_async_copy(gate_hbm.at[at], gate_v.at[at], sems.at[i, 0]),
            pltpu.make_async_copy(up_hbm.at[at], up_v.at[at], sems.at[i, 1]),
        )

    for i in range(blocks):
        for copy in copies(i):
            copy.start()

    def step(i, carry):
        for copy in copies(i):
            copy.wait()
        at = pl.ds(pl.multiple_of(i * block, block), block)
        acc = mm(rel[:, :width], gate_v[at, :], 1, 1) + mm(rel[:, width:], up_v[at, :], 1, 1)
        rows = acc.shape[0] // SIDE
        for k, out in enumerate((o0, o1, o2, o3)):
            out[:, at] = acc[k * rows:(k + 1) * rows].astype(out.dtype)
        return carry

    lax.fori_loop(0, blocks, step, 0)


def stack_kernel(own, a, b, c, out):
    for k, block in enumerate((own, a, b, c)):
        out[k] = block[...]


def sum_kernel(own, a, c, b, out):
    total = (own[...].astype(F32) + b[...].astype(F32)) + (a[...].astype(F32) + c[...].astype(F32))
    out[...] = total.astype(out.dtype)


def copy_kernel(one, out):
    out[...] = one[...]


def add_kernel(one, two, out):
    out[...] = (one[...].astype(F32) + two[...].astype(F32)).astype(out.dtype)


def column_block(pos, j, k):
    first, second = (pos[0] + SIDE - k) % SIDE, (pos[1] + SIDE - j) % SIDE
    return jnp.where(pos[2] == 0, second * SIDE + first, first * SIDE + second)


def place_rows(steps, pos, blocks, out, sems):
    rows = blocks[0].shape[0]
    copies = []
    for i, k in enumerate(steps):
        at = (pos[0] + SIDE - k) % SIDE
        at = pl.ds(pl.multiple_of(at * rows, rows), rows)
        copies.append(pltpu.make_async_copy(blocks[i], out.at[at], sems.at[i]))
        copies[-1].start()
    return copies


def put_rows(steps, pos, blocks, so_far):
    n = len(blocks)

    def kernel(pos, *refs):
        for copy in place_rows(steps, pos, refs[:n], refs[n + 1], refs[n + 2]):
            copy.wait()

    return pl.pallas_call(
        kernel,
        in_specs=[smem()] + [vmem()] * n + [hbm()],
        out_specs=hbm(),
        out_shape=shape(*so_far.shape),
        scratch_shapes=[pltpu.SemaphoreType.DMA((n,))],
        input_output_aliases={1 + n: 0},
        compiler_params=pltpu.CompilerParams(vmem_limit_bytes=MIB),
        cost_estimate=cost("rows"),
    )(pos, *blocks, so_far)


def left_kernel(pos, z_t, t0, t1, t3, t2, keep, send, whole):
    half, r = keep.shape[0], keep.shape[1]
    for j, stack in enumerate((t0, t1, t2, t3)):
        for k in range(SIDE):
            part = mm(z_t[...], stack[k], 1, 0)
            whole[column_block(pos, j, k)] = part[:r] + part[r:]
    keep[...] = whole[pl.ds(pos[2] * half, half)]
    send[...] = whole[pl.ds((1 - pos[2]) * half, half)].astype(send.dtype)


def turn_kernel(pos, t0, t1, t3, t2, out):
    for j, stack in enumerate((t0, t1, t2, t3)):
        for k in range(SIDE):
            out[column_block(pos, j, k)] = stack[k].T


def right_kernel(pos, mine, other, gate, t0, t1, t3, t2, left, keep, send, gram):
    half, r = mine.shape[0], mine.shape[1]
    left[pl.ds(pos[2] * half, half)] = mine[...]
    left[pl.ds((1 - pos[2]) * half, half)] = other[...]
    w = jnp.zeros((gate.shape[0], r), F32)
    c = jnp.zeros((r, r), F32)
    for j, stack in enumerate((t0, t1, t2, t3)):
        for k in range(SIDE):
            piece = left[column_block(pos, j, k)]
            w = w + mm(stack[k], piece, 1, 1)
            c = c + mm(piece, piece, 1, 1)
    gram[...] = c
    w_hi, w_lo = split_hi_lo(w)
    v = mm(jnp.concatenate([w_hi, w_lo], 1), gate[...], 0, 0)
    v = v[:r] + v[r:]
    low, high = v[:r // 2], v[r // 2:]
    keep[...] = jnp.where(pos[2] == 0, low, high)
    send[...] = jnp.where(pos[2] == 0, high, low)


def eliminate(a, steps):
    row_id = lax.broadcasted_iota(jnp.int32, (a.shape[0], 1), 0)
    for k in steps:
        row = a[k:k + 1, :]
        scale = jnp.where(row_id > k, a[:, k:k + 1] / a[k:k + 1, k:k + 1], 0.0)
        a = a - scale * row
    return a


def diagonal(r, shift):
    row_id = lax.broadcasted_iota(jnp.int32, (r, 2 * r), 0)
    return row_id + shift == lax.broadcasted_iota(jnp.int32, (r, 2 * r), 1)


def cholesky_kernel(gram, out):
    r = gram.shape[0]
    eye = jnp.where(diagonal(r, r), 1.0, 0.0).astype(F32)
    a = jnp.concatenate([gram[...], jnp.zeros((r, r), F32)], 1) + eye
    out[...] = eliminate(a, range(r * 11 // 16))


def inverse_kernel(half, left, out, left_n):
    r = half.shape[0]
    a = eliminate(half[...], range(r * 11 // 16, r))
    diag = jnp.sum(jnp.where(diagonal(r, 0), a, 0.0), axis=1, keepdims=True)
    out[...] = a[:, r:] / jnp.sqrt(diag)
    for s in range(left.shape[0]):
        left_n[s] = jnp.concatenate([left[s], left[s]], 0).T


def residual_kernel(
    n_dp, pos, mine, other, inv, gate, left_n, turned, quarter,
    gate_q_t, out_hbm, grad_input, right, out, sems, row_sems,
):
    own_rows = place_rows((0,), pos, (quarter,), grad_input, row_sems)
    low = jnp.where(pos[2] == 0, mine[...], other[...])
    high = jnp.where(pos[2] == 0, other[...], mine[...])
    v_t = jnp.concatenate([low, high], 0)
    r = v_t.shape[0]
    q = mm_exact(inv[...], v_t, 1, 0) * (1.0 / n_dp)
    gate_q_t[...] = q
    hi, lo = split_hi_lo(-mm_exact(inv[...], q, 0, 0))
    right[:r] = hi
    right[r:] = lo
    blocks = sems.shape[0]
    slots, cols = turned.shape[0], turned.shape[1]
    each = slots // blocks
    rows = each * cols
    copies = []
    for i in range(blocks):
        for s in range(i * each, (i + 1) * each):
            out[s * cols:(s + 1) * cols, :] = (
                mm(turned[s], gate[...], 1, 0) + mm(left_n[s], right[...], 1, 0)
            ).astype(out.dtype)
        at = pl.ds(i * rows, rows)
        copies.append(pltpu.make_async_copy(out.at[at], out_hbm.at[at], sems.at[i]))
        copies[-1].start()
    for copy in copies + own_rows:
        copy.wait()


def residual(pos, mine, other, inv, gate, left_n, turned, quarter, n_dp):
    tokens, width = gate.shape
    n, cols, twice = left_n.shape
    d = n * cols
    blocks = 8
    return pl.pallas_call(
        lambda *refs: residual_kernel(n_dp, *refs),
        in_specs=[smem()] + [vmem()] * 7,
        out_specs=[vmem(), hbm(), hbm()],
        out_shape=[shape(twice // 2, width, dtype=F32), shape(d, width), shape(tokens, d)],
        scratch_shapes=[
            pltpu.VMEM((twice, width), BF16),
            pltpu.VMEM((d, width), BF16),
            pltpu.SemaphoreType.DMA((blocks,)),
            pltpu.SemaphoreType.DMA((1,)),
        ],
        compiler_params=pltpu.CompilerParams(vmem_limit_bytes=32 * MIB),
        cost_estimate=cost("residual"),
    )(pos, mine, other, inv, gate, left_n, turned, quarter)


def plane(n_dp, first, shift):
    pairs = []
    for i in range(n_dp):
        along_x = (i % 2 == 0) == first
        for y in range(SIDE):
            for x in range(SIDE):
                to = (y, (x + shift) % SIDE) if along_x else ((y + shift) % SIDE, x)
                n = SIDE * SIDE
                pairs.append((i * n + y * SIDE + x, i * n + to[0] * SIDE + to[1]))
    return pairs


def ring_pairs(n_dp, step):
    pairs = []
    for i in range(n_dp):
        z, core = i // 2, i % 2
        partner = z ^ 1 if core == step else SIDE - 1 - z
        pairs.append((i, partner * 2 + core))
    return pairs


def local(tokens, gate_pre, up_act, grad_hidden, gate_weight, up_weight, q_init):
    n_dp = lax.axis_size("dp")
    me = lax.axis_index("tensor")
    x, y = me % SIDE, me // SIDE
    core = lax.axis_index("dp") % 2
    a, b = jnp.where(core == 0, x, y), jnp.where(core == 0, y, x)
    pos = jnp.stack([a, b, core]).astype(jnp.int32)
    t_tok, width = gate_pre.shape
    r = q_init.shape[1]
    d = gate_weight.shape[0]
    n = SIDE * SIDE
    cols = d // n

    def over_first(a, k):
        return lax.ppermute(a, ("dp", "tensor"), plane(n_dp, True, k))

    def over_second(a, j):
        return lax.ppermute(a, ("dp", "tensor"), plane(n_dp, False, j))

    def over_ring(a, step):
        return lax.ppermute(a, "dp", ring_pairs(n_dp, step))

    def over_core(a):
        return lax.ppermute(a, "dp", [(i, i ^ 1) for i in range(n_dp)])

    shifts = (1, 3, 2)
    act = pltpu.VMEM((t_tok, width), BF16)
    weights = pltpu.VMEM((d, width), BF16)

    def add(name, one, two, out, after=()):
        return call(name, add_kernel, out, [one, two], after=after)

    got = {k: over_first(tokens, k) for k in shifts}
    gate, rel, z_t, own = call(
        "gates", gates_kernel,
        [shape(t_tok, width), shape(t_tok, 2 * width), shape(2 * r, t_tok), shape(t_tok, cols)],
        [(hbm(), a) for a in (gate_pre, up_act, grad_hidden, q_init.T, tokens)],
        scratch=[act, act, act, pltpu.VMEM((r, width), F32), pltpu.SemaphoreType.DMA((5,))],
        mib=60,
    )
    own = call("own", copy_kernel, shape(t_tok, cols), [own])
    stack0 = call(
        "stack", stack_kernel, shape(SIDE, t_tok, cols), [own, got[1], got[2], got[3]]
    )
    far = {j: over_second(stack0, j) for j in shifts}
    stacks = [stack0, far[1], far[3], far[2]]

    parts = call(
        "partial", partial_kernel,
        [shape(t_tok // SIDE, d, dtype=F32)] + [shape(t_tok // SIDE, d)] * 3,
        [rel, (hbm(), gate_weight), (hbm(), up_weight)],
        scratch=[weights, weights, pltpu.SemaphoreType.DMA((8, 2))], mib=48, after=[stack0],
    )
    got = {k: over_first(parts[k], k) for k in shifts}

    part_left = shape(n // 2, r, cols)
    keep, send = call(
        "left", left_kernel, [shape(n // 2, r, cols, dtype=F32), part_left],
        [z_t, *stacks],
        scratch=[pltpu.VMEM((n, r, cols), F32)], pos=pos, after=[parts[0]],
    )
    pair = add("pair0", keep, over_core(send), part_left)
    near = over_ring(pair, 0)
    turned = call("turn", turn_kernel, shape(n, cols, t_tok), stacks, pos=pos, after=[pair])
    sums = call(
        "sums", sum_kernel, shape(t_tok // SIDE, d), [parts[0], got[1], got[3], got[2]],
        after=[turned],
    )
    got = {j: over_second(sums, j) for j in shifts}
    pair = add("pair1", pair, near, part_left, after=[sums])
    near = over_ring(pair, 1)
    mine = add("mine", pair, near, part_left)
    other = over_core(mine)
    left, keep, send, gram = call(
        "right", right_kernel,
        [shape(n, r, cols)] + [shape(r // 2, width, dtype=F32)] * 2 + [shape(r, r, dtype=F32)],
        [mine, other, gate, *stacks], pos=pos,
    )

    part_right = shape(r // 2, width, dtype=F32)
    pair = add("pair2", keep, over_core(send), part_right)
    near = over_ring(pair, 0)
    half = call("cholesky", cholesky_kernel, shape(r, 2 * r, dtype=F32), [gram], after=[pair])
    pair = add("pair3", pair, near, part_right, after=[half])
    near = over_ring(pair, 1)
    quarter = call(
        "quarter", sum_kernel, shape(t_tok // SIDE, d), [sums, got[1], got[3], got[2]],
        after=[pair],
    )
    got = {k: over_first(quarter, k) for k in shifts}
    inv, left_n = call(
        "inverse", inverse_kernel, [shape(r, r, dtype=F32), shape(n, cols, 2 * r)], [half, left],
        after=[quarter],
    )
    mine = add("mine2", pair, near, part_right, after=[inv])
    other = over_core(mine)
    gate_q_t, error, rows = residual(pos, mine, other, inv, gate, left_n, turned, quarter, n_dp)
    grad_input = put_rows((2, 1, 3), pos, [got[k] for k in (2, 1, 3)], rows)
    return (grad_input, gate_q_t.T, error)


def solution(mesh):
    return jax.shard_map(
        local,
        mesh=mesh,
        in_specs=(
            P("dp", "tensor"),
            P("dp", "tensor"),
            P("dp", "tensor"),
            P("dp", "tensor"),
            P(None, "tensor"),
            P(None, "tensor"),
            P("tensor", None),
        ),
        out_specs=(P("dp", None), P("tensor", None), P("dp", "tensor")),
        check_vma=False,
    )
```
